512 devices in a mesh: ctx: 64 (over z, y), fsdp: 8 (over x, core).
Axes of the slice: x: 4, y: 8, z: 8, core: 2. Of those that a mesh axis runs over, the one named last changes fastest.
Arguments:
- tokens: bfloat16 [32768, 4608], P('ctx'), may hold values from -40 to 40
- w_query: bfloat16 [4608, 2048], P('ctx', 'fsdp'), may hold values from -0.1 to 0.1
- w_key: bfloat16 [4608, 1024], P('ctx', 'fsdp'), may hold values from -0.1 to 0.1
- w_value: bfloat16 [4608, 1024], P('ctx', 'fsdp'), may hold values from -0.09375 to 0.09375
- doc_ids: int32 [32768], replicated, may hold values from 0 to 15, never falling along the last dimension, each value on 1 to 8192 neighbouring positions
Outputs:
- attended: bfloat16 [32768, 2048], P(('ctx', 'fsdp'))
The draws below stay inside these ranges and needn't reach their ends.
Inputs may be any that keep to these rules, and one draw needn't show every extreme that they name: `doc_ids`: document numbers start at 0, never fall along the sequence, and each document spans 1 to 8192 consecutive positions; one spans exactly 8192.
All inputs are finite; a program needn't handle non-finite values.
Results may differ from the reference program's by a relative error of at most 0.007.
Values may be sent and summed in bfloat16 or wider, within the bound.
A program may use at most 64 MiB of HBM per device.

```python
import math
import jax
import jax.numpy as jnp
import numpy as np
from jax import lax

D = 4608
H = 16
KV = 8
HD = 128
WINDOW = 4096
CTX_TOK = 512
SEQ = 32768


weight_edge = 0.099609375


def draw_w_query(key, part):
    own_part = jax.random.normal(jax.random.fold_in(key, 102), (D, KV, H // KV, HD), jnp.float32)
    mixed = own_part
    scaled = jnp.clip(mixed * D ** (-0.5), -weight_edge, weight_edge)
    return scaled.reshape(D, H * HD).astype(jnp.bfloat16)


def draw_w_key(key, part):
    own_part = jax.random.normal(jax.random.fold_in(key, 103), (D, KV, HD), jnp.float32)
    mixed = own_part
    scaled = jnp.clip(mixed * D ** (-0.5), -weight_edge, weight_edge)
    return scaled.reshape(D, KV * HD).astype(jnp.bfloat16)


def draw_tokens(key, part):
    values = jax.random.normal(jax.random.fold_in(key, 107), (SEQ, D), jnp.float32)
    return jnp.clip(values, -40.0, 40.0).astype(jnp.bfloat16)


def shard_levels(rng, shape, cuts, low, largest):
    level = 1.0
    for position, shards_of in cuts:
        steps = jax.random.uniform(jax.random.fold_in(jax.random.fold_in(rng, 6), position), (shards_of,), jnp.float32, low / len(cuts), largest / len(cuts))
        level = level * jnp.repeat(jnp.exp(steps), shape[position] // shards_of).reshape((-1,) + (1,) * (len(shape) - 1 - position))
    return level


def length_profile(count, total, bound, lean):
    portions = [(1 << 20) // math.isqrt(rank ** lean) + 1 for rank in range(2, count + 1)]
    surplus, holding = total - bound - (count - 1), [1] * (count - 1)
    while surplus > 0:
        free = [i for i in range(count - 1) if holding[i] < bound]
        whole, left = sum([portions[i] for i in free]), surplus
        for i in free:
            addition = min(bound - holding[i], max(1, left * portions[i] // whole), surplus)
            holding[i] = holding[i] + addition
            surplus = surplus - addition
    return np.array([bound] + holding)


def ragged(key, amount, total, reach, lean):
    if amount == 2:
        one = jax.random.randint(key, (), max(1, total - reach), min(reach, total - 1) + 1)
        return jnp.stack([one, total - one])
    sizes = jnp.asarray(length_profile(amount, total, reach, lean), jnp.int32)
    pairs = (amount - 1) // 2
    source_of, receiver = sizes[1:1 + 2 * pairs:2], sizes[2:2 + 2 * pairs:2]
    room = jnp.minimum(source_of - 1, reach - receiver)
    shifted = jax.random.randint(jax.random.fold_in(key, 1), (pairs,), 0, 1 << 20) % (room + 1)
    sizes = sizes.at[1:1 + 2 * pairs:2].set(source_of - shifted).at[2:2 + 2 * pairs:2].set(receiver + shifted)
    return sizes[jax.random.permutation(jax.random.fold_in(key, 2), amount)]


def centred(rng, extent, scale, bound, shards=(), kind=jnp.bfloat16):
    loudness = shard_levels(rng, extent, shards, -0.22, 0.18) if shards else 1.0
    values = jax.random.normal(rng, extent, jnp.float32) * scale * loudness
    return jnp.minimum(jnp.maximum(values, -bound), bound).astype(kind)


def setup_inputs(seed: int = 0) -> dict:
    key_of = jax.random.split(jax.random.key(seed), 6)
    tokens = draw_tokens(jax.random.fold_in(key_of[5], 71), 0)
    w_query = draw_w_query(jax.random.fold_in(key_of[5], 71), 0)
    w_key = draw_w_key(jax.random.fold_in(key_of[5], 71), 0)
    w_value = centred(key_of[3], (D, KV * HD), D ** -0.5, 0.09375, ((0, 64), (1, 8)))
    doc_ids = jnp.searchsorted(jnp.cumsum(ragged(key_of[4], SEQ // (4 * CTX_TOK), SEQ, 2 * WINDOW, 2)), jnp.arange(SEQ), side="right").astype(jnp.int32)
    return {"tokens": tokens, "w_query": w_query, "w_key": w_key, "w_value": w_value, "doc_ids": doc_ids}


query_scale = 144.0 ** -0.5
score_cap = 50.0


def reference(tokens, w_query, w_key, w_value, doc_ids):
    queries = jnp.dot(tokens, w_query, preferred_element_type=jnp.float32).astype(jnp.bfloat16)
    keys = jnp.dot(tokens, w_key, preferred_element_type=jnp.float32).astype(jnp.bfloat16)
    values = jnp.dot(tokens, w_value, preferred_element_type=jnp.float32).astype(jnp.bfloat16)
    group_size = H // KV
    span = WINDOW + CTX_TOK
    padded_keys = jnp.concatenate([jnp.zeros((WINDOW, KV * HD), jnp.bfloat16), keys], axis=0)
    padded_values = jnp.concatenate([jnp.zeros((WINDOW, KV * HD), jnp.bfloat16), values], axis=0)
    padded_docs = jnp.concatenate([jnp.full((WINDOW,), -1, jnp.int32), doc_ids.astype(jnp.int32)], axis=0)

    def one_block(block_index):
        first_row = (block_index * CTX_TOK).astype(jnp.int32)
        query_blk = lax.dynamic_slice_in_dim(queries, first_row, CTX_TOK, 0).astype(jnp.float32)
        query_blk = query_blk.reshape(CTX_TOK, KV, group_size, HD)
        key_blk = lax.dynamic_slice_in_dim(padded_keys, first_row, span, 0).astype(jnp.float32).reshape(span, KV, HD)
        value_blk = lax.dynamic_slice_in_dim(padded_values, first_row, span, 0).astype(jnp.float32).reshape(span, KV, HD)
        query_doc = lax.dynamic_slice_in_dim(doc_ids.astype(jnp.int32), first_row, CTX_TOK, 0)
        key_doc = lax.dynamic_slice_in_dim(padded_docs, first_row, span, 0)
        query_pos = first_row + jnp.arange(CTX_TOK, dtype=jnp.int32)
        key_pos = first_row - WINDOW + jnp.arange(span, dtype=jnp.int32)
        distance = query_pos[:, None] - key_pos[None, :]
        visible = (query_doc[:, None] == key_doc[None, :]) & (distance >= 0) & (distance < WINDOW) & (key_pos[None, :] >= 0)
        scores = jnp.einsum("cngd,lnd->ngcl", query_blk, key_blk) * query_scale
        scores = score_cap * jnp.tanh(scores / score_cap)
        expo = jnp.where(visible, jnp.exp(scores), 0.0)
        denom = jnp.sum(expo, axis=-1)
        rounded = lax.optimization_barrier(expo.astype(jnp.bfloat16)).astype(jnp.float32)
        result = jnp.einsum("ngcl,lnd->ngcd", rounded, value_blk) / denom[..., None]
        return result.transpose(2, 0, 1, 3).reshape(CTX_TOK, H * HD).astype(jnp.bfloat16)

    blocks = lax.map(one_block, jnp.arange(SEQ // CTX_TOK, dtype=jnp.int32))
    return blocks.reshape(SEQ, H * HD)
```

```python
import functools
import math

import jax
import jax.numpy as jnp
from jax import lax
from jax.experimental import pallas as pl
from jax.experimental.pallas import tpu as pltpu
from jax.sharding import PartitionSpec as P

MESH = pl.DeviceIdType.MESH
HD = 128
WINDOW = 4096
SHARD = 512
D = 4608
SLAB = 72
NZ = NY = 8
NF = 8
BF = jnp.bfloat16
F32 = jnp.float32

query_scale = 144.0 ** (-0.5)
score_cap = 50.0
IN_SCALE = query_scale / score_cap
OUT_SCALE = score_cap * math.log2(math.e)


def kernel(tok_hbm, wq_hbm, wk_hbm, wv_hbm, doc_ref, out_ref,
           tok, wk, wv, wq, kvs, q, acc, oacc, dacc, lower, att,
           loc_sem, k1s, k1r, v1s, v1r, k2s, k2r, v2s, v2r, q1s, q1r, q2s, q2r,
           hzs, hs, hr, as_, ar):
    c = lax.axis_index("ctx")
    f = lax.axis_index("fsdp")
    z, y = c // NY, c % NY

    def at(zz, yy):
        return (lax.rem(zz + NZ, NZ) * NY + lax.rem(yy + NY, NY), f)

    def remote(src, dst, ssem, rsem, dev):
        return pltpu.make_async_remote_copy(
            src_ref=src, dst_ref=dst, send_sem=ssem, recv_sem=rsem,
            device_id=dev, device_id_type=MESH)

    sent = []

    def go(copy):
        copy.start()
        sent.append(copy)

    own_q0 = pltpu.make_async_copy(wq_hbm.at[:, pl.ds(0, HD)], wq.at[0, z, y], loc_sem.at[0])
    own_q1 = pltpu.make_async_copy(wq_hbm.at[:, pl.ds(HD, HD)], wq.at[1, z, y], loc_sem.at[1])
    own_k = pltpu.make_async_copy(wk_hbm, wk.at[z, y], loc_sem.at[2])
    own_v = pltpu.make_async_copy(wv_hbm, wv.at[y, z], loc_sem.at[3])
    own_tok = pltpu.make_async_copy(tok_hbm, tok, loc_sem.at[4])
    own_k.start()
    own_v.start()
    own_q0.start()
    own_q1.start()
    own_tok.start()

    bar = pltpu.get_barrier_semaphore()
    peers = [at(z, y + d) for d in range(1, NY)]
    peers += [at(z + d, y) for d in range(1, NZ)]
    peers += [(c, lax.rem(f + d, NF)) for d in range(1, NF)]
    for p in peers:
        pl.semaphore_signal(bar, inc=1, device_id=p, device_id_type=MESH)

    @pl.when(y == NY - 1)
    def _():
        pl.semaphore_signal(bar, inc=1, device_id=at(z + 1, 0), device_id_type=MESH)

    @pl.when(y == 0)
    def _():
        pl.semaphore_signal(bar, inc=1, device_id=at(z - 1, NY - 1), device_id_type=MESH)

    edge = jnp.where((y == 0) | (y == NY - 1), 1, 0)
    pl.semaphore_wait(bar, len(peers) + edge)

    own_k.wait()
    own_v.wait()
    order = [1, 7, 2, 6, 3, 5, 4]
    for d in order:
        go(remote(wk.at[z, y], wk.at[z, y], k1s.at[d], k1r.at[d], at(z, y + d)))
        go(remote(wv.at[y, z], wv.at[y, z], v1s.at[d], v1r.at[d], at(z + d, y)))
    own_q0.wait()
    own_q1.wait()

    def q_first(s):
        for side in (0, 1):
            sign = 1 - 2 * side
            if s > (4 if side == 0 else 3):
                continue
            src = lax.rem(y - sign * (s - 1) + NY, NY)
            if s > 1:
                remote(wq.at[:, z, src], wq.at[:, z, src], q1s.at[side, s - 1], q1r.at[side, s - 1], at(z, y)).wait_recv()
            go(remote(wq.at[:, z, src], wq.at[:, z, src], q1s.at[side, s], q1r.at[side, s], at(z, y + sign)))

    def q_first_done():
        for side, s in ((0, 4), (1, 3)):
            sign = 1 - 2 * side
            src = lax.rem(y - sign * s + NY, NY)
            remote(wq.at[:, z, src], wq.at[:, z, src], q1s.at[side, s], q1r.at[side, s], at(z, y)).wait_recv()

    docs = doc_ref[...]
    half = doc_ref[pl.ds(pl.multiple_of((c // 2) * 8, 8), 8), :]
    starts = jnp.zeros((8, 128), jnp.int32)
    for n in range(1, 16):
        begin = jnp.sum((docs < n).astype(jnp.int32))
        starts = jnp.where(half == n, begin, starts)
    row = lax.broadcasted_iota(jnp.int32, (8, 128), 0)
    lane = lax.broadcasted_iota(jnp.int32, (8, 128), 1)
    pos = (c // 2) * (2 * SHARD) + row * 128 + lane
    starts = jnp.maximum(starts, pos - (WINDOW - 1))
    starts = jnp.where(c % 2 == 0, starts, jnp.concatenate([starts[4:8], starts[0:4]], axis=0))
    for r in range(4):
        wide = jnp.broadcast_to(starts[r:r + 1, :], (128, 128))
        lower[pl.ds(r * 128, 128), :] = jnp.transpose(wide)
    oacc[...] = jnp.zeros_like(oacc)
    dacc[...] = jnp.zeros_like(dacc)

    for d in order:
        src = lax.rem(y - d + NY, NY)
        remote(wk.at[z, src], wk.at[z, src], k1s.at[d], k1r.at[d], at(z, y)).wait_recv()
        src = lax.rem(z - d + NZ, NZ)
        remote(wv.at[y, src], wv.at[y, src], v1s.at[d], v1r.at[d], at(z, y)).wait_recv()

    def ring(buf, ssem, rsem, me, towards, side, s, piece):
        sign = 1 - 2 * side
        src = lax.rem(me - sign * (s - 1) + 8, 8)
        part = pl.ds(4 * piece, 4)
        return remote(buf.at[src, part], buf.at[src, part], ssem.at[side, s, piece], rsem.at[side, s, piece], towards(sign))

    def along_z(sign):
        return at(z + sign, y)

    def along_y(sign):
        return at(z, y + sign)

    def arrived(buf, ssem, rsem, me, towards, side, s, piece):
        sign = 1 - 2 * side
        src = lax.rem(me - sign * s + 8, 8)
        part = pl.ds(4 * piece, 4)
        remote(buf.at[src, part], buf.at[src, part], ssem.at[side, s, piece], rsem.at[side, s, piece], towards(sign)).wait_recv()

    streams = ((wk, k2s, k2r, z, along_z), (wv, v2s, v2r, y, along_y))

    def steps_of(side, piece):
        return 4 if side == piece else 3

    for s in range(1, 5):
        for piece in (0, 1):
            for side in (0, 1):
                for st in streams:
                    last = steps_of(side, piece)
                    if s > 1 and s - 1 <= last:
                        arrived(*st, side, s - 1, piece)
                    if s <= last:
                        go(ring(*st, side, s, piece))
        q_first(s)
    q_first_done()

    def q_stage(h, s):
        for piece in (0, 1):
            for side in (1, 0):
                last = 4 if side == 1 else 3
                args = (wq.at[h], q2s.at[h], q2r.at[h], z, along_z, side)
                if s > 1 and s - 1 <= last:
                    arrived(*args, s - 1, piece)
                if s <= last:
                    go(ring(*args, s, piece))

    q_stage(0, 1)
    for piece in (0, 1):
        side = piece
        for st in streams:
            arrived(*st, side, 4, piece)

    own_tok.wait()
    acc[...] = jnp.zeros_like(acc)

    def kv_dot(i, carry):
        ws = []
        for zz in (0, 1):
            for yy in range(8):
                kk = wk[2 * i + zz, yy].astype(F32)
                vv = wv[yy, 2 * i + zz].astype(F32)
                ws.append(jnp.concatenate([kk, vv], axis=1))
        w = jnp.concatenate(ws, axis=0).astype(BF)
        t = tok[:, pl.ds(pl.multiple_of(i * 1152, 1152), 1152)]
        acc[...] += jnp.dot(t, w, preferred_element_type=F32)
        return carry

    lax.fori_loop(0, 4, kv_dot, 0)
    kvs[0] = acc[...].astype(BF)

    def reach(yy):
        yy = lax.rem(yy + NY, NY)
        return 3 + jnp.where(yy >= 4, 1, 0) + jnp.where(yy == 7, 1, 0) - jnp.where(yy == 0, 1, 0)

    mine, nxt, prv = reach(y), reach(y + 1), reach(y - 1)
    right = (lax.rem(jnp.where(y == 7, c + 1, c + 1) + 64, 64), f)
    left = (lax.rem(c - 1 + 64, 64), f)

    def halo(src_slot, dst_slot, piece, side, dev):
        part = pl.ds(256 * piece, 256)
        return remote(kvs.at[src_slot, part], kvs.at[dst_slot, part], hs.at[side, dst_slot, piece], hr.at[dst_slot, piece], dev)

    def halo_wait(slot, piece):
        halo(slot, slot, piece, 0, at(z, y)).wait_recv()

    for piece in (0, 1):
        part = pl.ds(256 * piece, 256)
        go(remote(kvs.at[0, part], kvs.at[8, part], hzs.at[piece], hr.at[8, piece], at(z + 1, y)))

        @pl.when(y != 7)
        def _():
            halo(0, 1, piece, 0, at(z, y + 1)).start()

        @pl.when(y == 0)
        def _():
            halo(0, 7, piece, 1, at(z, y - 1)).start()

    def halo_first():
        for piece in (0, 1):
            halo_wait(8, piece)

            @pl.when(y == 7)
            def _():
                halo(8, 1, piece, 0, at(z, y + 1)).start()

            @pl.when(y != 0)
            def _():
                halo(8, 7, piece, 1, at(z, y - 1)).start()

    def halo_right(slot, ok):
        for piece in (0, 1):
            @pl.when(ok)
            def _():
                halo_wait(slot, piece)

                @pl.when(slot + 1 <= nxt)
                def _():
                    halo(slot, slot + 1, piece, 0, right).start()

    def halo_left(slot, ok):
        for piece in (0, 1):
            @pl.when(ok)
            def _():
                halo_wait(slot, piece)

                @pl.when(9 - slot <= 7 - prv)
                def _():
                    halo(slot, slot - 1, piece, 1, left).start()

    slot_a = jnp.where(mine == 2, 5, 3)
    slot_b = jnp.where((mine == 3) | (mine == 4), 5, 4)
    slot_c = 12 - slot_a - slot_b

    lane_id = lax.broadcasted_iota(jnp.int32, (1, 128), 1)

    def attend(h, slot):
        base = (c - slot) * SHARD

        def tile(i, carry):
            rows = pl.ds(pl.multiple_of(i * 256, 256), 256)
            s = lax.dot_general(q[h, rows, :], kvs[slot, :, pl.ds(0, HD)],
                                (((1,), (1,)), ((), ())), preferred_element_type=F32)
            low = lower[rows, :] - base
            den = dacc[h, rows, :]
            parts = []
            for t in range(4):
                e = jnp.exp2(jnp.tanh(s[:, t * 128:(t + 1) * 128] * IN_SCALE) * OUT_SCALE)
                e = jnp.where(lane_id + t * 128 >= low, e, 0.0)
                den += e
                parts.append(e.astype(BF))
            dacc[h, rows, :] = den
            p = jnp.concatenate(parts, axis=1)
            oacc[h, rows, :] += jnp.dot(p, kvs[slot, :, pl.ds(HD, HD)], preferred_element_type=F32)
            return carry

        lax.fori_loop(0, 2, tile, 0)

    def attend_own(h):
        for i in range(4):
            n = i + 1
            rows = pl.ds(i * 128, 128)
            s = lax.dot_general(q[h, rows, :], kvs[0, pl.ds(0, n * 128), pl.ds(0, HD)],
                                (((1,), (1,)), ((), ())), preferred_element_type=F32)
            low = lower[rows, :] - c * SHARD
            den = dacc[h, rows, :]
            parts = []
            for t in range(n):
                e = jnp.exp2(jnp.tanh(s[:, t * 128:(t + 1) * 128] * IN_SCALE) * OUT_SCALE)
                seen = lane_id + t * 128 >= low
                if t == i:
                    seen = seen & (lane_id <= lax.broadcasted_iota(jnp.int32, (128, 128), 0))
                e = jnp.where(seen, e, 0.0)
                den += e
                parts.append(e.astype(BF))
            dacc[h, rows, :] = den
            p = jnp.concatenate(parts, axis=1) if n > 1 else parts[0]
            oacc[h, rows, :] += jnp.dot(p, kvs[0, pl.ds(0, n * 128), pl.ds(HD, HD)], preferred_element_type=F32)

    def q_dot(h):
        cols = pl.ds(0, HD)
        acc[:, cols] = jnp.zeros((SHARD, HD), F32)

        def step(i, carry):
            ws = []
            for zz in (0, 1):
                for yy in range(8):
                    ws.append(wq[h, 2 * i + zz, yy].astype(F32))
            w = jnp.concatenate(ws, axis=0).astype(BF)
            t = tok[:, pl.ds(pl.multiple_of(i * 1152, 1152), 1152)]
            acc[:, cols] += jnp.dot(t, w, preferred_element_type=F32)
            return carry

        lax.fori_loop(0, 4, step, 0)
        q[h] = acc[:, cols].astype(BF)

    def finish(h):
        den = jnp.sum(dacc[h], axis=1, keepdims=True)
        att[h] = (oacc[h] / den).astype(BF)
        for d in range(1, NF):
            peer = lax.rem(f + d, NF)
            rows = pl.ds(pl.multiple_of(peer * 64, 64), 64)
            cols = pl.ds(pl.multiple_of(f * 256 + h * HD, HD), HD)
            go(remote(att.at[h, rows], out_ref.at[:, cols], as_.at[h, d], ar.at[h, d], (c, peer)))
        rows = pl.ds(pl.multiple_of(f * 64, 64), 64)
        cols = pl.ds(pl.multiple_of(f * 256 + h * HD, HD), HD)
        pltpu.make_async_copy(att.at[h, rows], out_ref.at[:, cols], loc_sem.at[h]).start()

    def finish_wait(h):
        rows = pl.ds(pl.multiple_of(f * 64, 64), 64)
        for d in range(1, NF):
            peer = lax.rem(f - d + NF, NF)
            cols = pl.ds(pl.multiple_of(peer * 256 + h * HD, HD), HD)
            remote(att.at[h, rows], out_ref.at[:, cols], as_.at[h, d], ar.at[h, d], (c, f)).wait_recv()
        cols = pl.ds(pl.multiple_of(f * 256 + h * HD, HD), HD)
        pltpu.make_async_copy(att.at[h, rows], out_ref.at[:, cols], loc_sem.at[h]).wait()

    q_stage(0, 2)
    halo_first()
    halo_right(1, mine >= 1)
    q_stage(0, 3)
    q_stage(0, 4)
    q_stage(1, 1)
    halo_left(7, mine <= 6)
    halo_right(2, mine >= 2)
    q_stage(0, 5)
    q_dot(0)
    attend_own(0)
    q_stage(1, 2)
    attend(0, 8)
    attend(0, 1)
    halo_left(6, mine <= 5)
    halo_left(slot_a, mine == 2)
    halo_right(slot_a, mine != 2)
    q_stage(1, 3)
    lax.fori_loop(0, 3, lambda i, x: (attend(0, jnp.where(i == 0, 7, jnp.where(i == 1, 2, 6))), x)[1], 0)
    q_stage(1, 4)
    attend(0, slot_a)
    left_b = (mine <= 4)
    halo_left(slot_b, left_b)
    halo_right(slot_b, jnp.logical_not(left_b))
    attend(0, slot_b)
    q_stage(1, 5)
    q_dot(1)
    attend_own(1)

    def later(i, x):
        slot = jnp.where(i == 0, 8, jnp.where(i == 1, 1, jnp.where(i == 2, 7, jnp.where(
            i == 3, 2, jnp.where(i == 4, 6, jnp.where(i == 5, slot_a, slot_b))))))
        attend(1, slot)
        return x

    lax.fori_loop(0, 7, later, 0)
    left_c = (mine <= 3)
    halo_left(slot_c, left_c)
    halo_right(slot_c, jnp.logical_not(left_c))
    attend(0, slot_c)
    finish(0)
    attend(1, slot_c)
    finish(1)

    for copy in sent:
        copy.wait_send()
    for piece in (0, 1):
        halo(0, 1, piece, 0, right).wait_send()
        halo(0, 7, piece, 1, left).wait_send()
        for s in range(2, 6):
            @pl.when(s <= nxt)
            def _():
                halo(0, s, piece, 0, right).wait_send()

            @pl.when(s <= 7 - prv)
            def _():
                halo(0, 8 - s, piece, 1, left).wait_send()
    finish_wait(0)
    finish_wait(1)


def on_device(tokens, w_query, w_key, w_value, doc_ids):
    docs = doc_ids.reshape(256, 128)
    hbm = pl.BlockSpec(memory_space=pl.ANY)
    vmem = pl.BlockSpec(memory_space=pltpu.VMEM)
    dma = pltpu.SemaphoreType.DMA
    return pl.pallas_call(
        kernel,
        out_shape=jax.ShapeDtypeStruct((64, 2048), BF),
        in_specs=[hbm, hbm, hbm, hbm, vmem],
        out_specs=hbm,
        scratch_shapes=[
            pltpu.VMEM((SHARD, D), BF),
            pltpu.VMEM((8, 8, SLAB, HD), BF),
            pltpu.VMEM((8, 8, SLAB, HD), BF),
            pltpu.VMEM((2, 8, 8, SLAB, HD), BF),
            pltpu.VMEM((9, SHARD, 2 * HD), BF),
            pltpu.VMEM((2, SHARD, HD), BF),
            pltpu.VMEM((SHARD, 2 * HD), F32),
            pltpu.VMEM((2, SHARD, HD), F32),
            pltpu.VMEM((2, SHARD, HD), F32),
            pltpu.VMEM((SHARD, HD), jnp.int32),
            pltpu.VMEM((2, SHARD, HD), BF),
            dma((5,)),
            dma((8,)), dma((8,)), dma((8,)), dma((8,)),
            dma((2, 5, 2)), dma((2, 5, 2)), dma((2, 5, 2)), dma((2, 5, 2)),
            dma((2, 5)), dma((2, 5)),
            dma((2, 2, 5, 2)), dma((2, 2, 5, 2)),
            dma((2,)), dma((2, 9, 2)), dma((9, 2)),
            dma((2, 8)), dma((2, 8)),
        ],
        compiler_params=pltpu.CompilerParams(
            collective_id=0, has_side_effects=True, vmem_limit_bytes=48 << 20),
        cost_estimate=pl.CostEstimate(flops=5 * 10 ** 9, bytes_accessed=10 ** 7, transcendentals=9 * 10 ** 6),
    )(tokens, w_query, w_key, w_value, docs)


def solution(mesh):
    return jax.shard_map(
        on_device,
        mesh=mesh,
        in_specs=(P("ctx", None), P("ctx", "fsdp"), P("ctx", "fsdp"), P("ctx", "fsdp"), P()),
        out_specs=P(("ctx", "fsdp"), None),
        check_vma=False,
    )
```

```python
import functools
import math

import jax
import jax.numpy as jnp
from jax import lax
from jax.experimental import pallas as pl
from jax.experimental.pallas import tpu as pltpu
from jax.sharding import PartitionSpec as P

MESH = pl.DeviceIdType.MESH
HD = 128
WINDOW = 4096
SHARD = 512
D = 4608
SLAB = 72
NZ = NY = 8
NF = 8
BF = jnp.bfloat16
F32 = jnp.float32

query_scale = 144.0 ** (-0.5)
score_cap = 50.0
IN_SCALE = query_scale / score_cap
OUT_SCALE = score_cap * math.log2(math.e)

ORDER = (
    ('S',), ('F', 1), ('F', 2), ('W',), ('K', 1, 1), ('F', 3), ('K', 1, 0), ('K', 2, 1), ('K', 2, 0),
    ('F', 4), ('K', 3, 1), ('K', 3, 0), ('G',), ('Q', 0, 1, 1), ('Q', 0, 1, 0), ('K', 4, 1), ('Q', 1, 1, 0),
    ('K', 4, 0), ('Q', 0, 2, 0), ('K', 5, 1), ('Q', 1, 1, 1), ('K', 5, 0), ('Q', 0, 2, 1), ('P',), ('B', 0),
    ('Q', 1, 2, 1), ('B', 1), ('Q', 0, 3, 0), ('H', 8, 0), ('Q', 0, 4, 0), ('Q', 0, 3, 1), ('Q', 1, 3, 1),
    ('Q', 1, 2, 0), ('D',), ('H', 8, 1), ('H', 1, 0), ('H', 7, 0), ('Q', 0, 4, 1), ('Q', 1, 4, 1),
    ('Q', 1, 3, 0), ('Q', 0, 5, 0), ('H', 7, 1), ('H', 1, 1), ('Q', 0, 5, 1), ('R', 0), ('O', 0),
    ('H', 6, 0), ('A', 0, 8), ('H', 2, 0), ('A', 0, 1), ('Q', 1, 4, 0), ('H', 6, 1), ('A', 0, 7),
    ('H', 2, 1), ('A', 0, 6), ('Q', 1, 5, 1), ('A', 0, 2), ('H', 3, 0), ('Q', 1, 5, 0), ('R', 1), ('O', 1),
    ('H', 5, 0), ('A', 1, 6), ('A', 1, 8), ('H', 3, 1), ('A', 1, 3), ('A', 1, 2), ('H', 4, 0), ('A', 1, 7),
    ('H', 5, 1), ('A', 1, 1), ('A', 1, 5), ('A', 0, 3), ('H', 4, 1), ('A', 1, 4), ('A', 0, 4), ('A', 0, 5),
)


def kernel(tok_hbm, wq_hbm, wk_hbm, wv_hbm, doc_hbm, out_ref,
           doc_ref, tok, wk, wv, wq, kvs, q, acc, oacc, dacc, lower, att,
           loc_sem, k1s, k1r, v1s, v1r, k2s, k2r, v2s, v2r, q1s, q1r, q2s, q2r,
           hs, hr, as_, ar):
    c = lax.axis_index("ctx")
    f = lax.axis_index("fsdp")
    z, y = c // NY, c % NY

    def at(zz, yy):
        return (lax.rem(zz + NZ, NZ) * NY + lax.rem(yy + NY, NY), f)

    def remote(src, dst, ssem, rsem, dev):
        return pltpu.make_async_remote_copy(
            src_ref=src, dst_ref=dst, send_sem=ssem, recv_sem=rsem,
            device_id=dev, device_id_type=MESH)

    sent = []

    def go(copy):
        copy.start()
        sent.append(copy)

    own_q0 = pltpu.make_async_copy(wq_hbm.at[:, pl.ds(0, HD)], wq.at[0, z, y], loc_sem.at[0])
    own_q1 = pltpu.make_async_copy(wq_hbm.at[:, pl.ds(HD, HD)], wq.at[1, z, y], loc_sem.at[1])
    own_k = pltpu.make_async_copy(wk_hbm, wk.at[z, y], loc_sem.at[2])
    own_v = pltpu.make_async_copy(wv_hbm, wv.at[y, z], loc_sem.at[3])
    own_doc = pltpu.make_async_copy(doc_hbm, doc_ref, loc_sem.at[5])
    own_tok = pltpu.make_async_copy(tok_hbm, tok, loc_sem.at[4])
    own_k.start()
    own_v.start()
    own_q0.start()
    own_q1.start()
    own_doc.start()
    own_tok.start()

    bar = pltpu.get_barrier_semaphore()
    peers = [at(z, y + d) for d in range(1, NY)]
    peers += [at(z + d, y) for d in range(1, NZ)]
    peers += [(c, lax.rem(f + d, NF)) for d in range(1, NF)]
    for p in peers:
        pl.semaphore_signal(bar, inc=1, device_id=p, device_id_type=MESH)

    @pl.when(y == NY - 1)
    def _():
        pl.semaphore_signal(bar, inc=1, device_id=at(z + 1, 0), device_id_type=MESH)

    @pl.when(y == 0)
    def _():
        pl.semaphore_signal(bar, inc=1, device_id=at(z - 1, NY - 1), device_id_type=MESH)

    edge = jnp.where((y == 0) | (y == NY - 1), 1, 0)
    pl.semaphore_wait(bar, len(peers) + edge)

    order = [1, 7, 2, 6, 3, 5, 4]

    def first_slabs():
        own_k.wait()
        own_v.wait()
        for d in order:
            go(remote(wk.at[z, y], wk.at[z, y], k1s.at[d], k1r.at[d], at(z, y + d)))
            go(remote(wv.at[y, z], wv.at[y, z], v1s.at[d], v1r.at[d], at(z + d, y)))
        own_q0.wait()
        own_q1.wait()
        oacc[...] = jnp.zeros_like(oacc)
        dacc[...] = jnp.zeros_like(dacc)

    def first_slabs_wait():
        for d in order:
            src = lax.rem(y - d + NY, NY)
            remote(wk.at[z, src], wk.at[z, src], k1s.at[d], k1r.at[d], at(z, y)).wait_recv()
            src = lax.rem(z - d + NZ, NZ)
            remote(wv.at[y, src], wv.at[y, src], v1s.at[d], v1r.at[d], at(z, y)).wait_recv()

    def q_first(s):
        for side in (0, 1):
            sign = 1 - 2 * side
            if s > (4 if side == 0 else 3):
                continue
            src = lax.rem(y - sign * (s - 1) + NY, NY)
            if s > 1:
                remote(wq.at[:, z, src], wq.at[:, z, src], q1s.at[side, s - 1], q1r.at[side, s - 1], at(z, y)).wait_recv()
            go(remote(wq.at[:, z, src], wq.at[:, z, src], q1s.at[side, s], q1r.at[side, s], at(z, y + sign)))

    def q_first_done():
        for side, s in ((0, 4), (1, 3)):
            sign = 1 - 2 * side
            src = lax.rem(y - sign * s + NY, NY)
            remote(wq.at[:, z, src], wq.at[:, z, src], q1s.at[side, s], q1r.at[side, s], at(z, y)).wait_recv()

    def bounds():
        own_doc.wait()
        docs = doc_ref[...]
        half = doc_ref[pl.ds(pl.multiple_of((c // 2) * 8, 8), 8), :]
        starts = jnp.zeros((8, 128), jnp.int32)
        for n in range(1, 16):
            begin = jnp.sum((docs < n).astype(jnp.int32))
            starts = jnp.where(half == n, begin, starts)
        row = lax.broadcasted_iota(jnp.int32, (8, 128), 0)
        lane = lax.broadcasted_iota(jnp.int32, (8, 128), 1)
        pos = (c // 2) * (2 * SHARD) + row * 128 + lane
        starts = jnp.maximum(starts, pos - (WINDOW - 1))
        starts = jnp.where(c % 2 == 0, starts, jnp.concatenate([starts[4:8], starts[0:4]], axis=0))
        for r in range(4):
            wide = jnp.broadcast_to(starts[r:r + 1, :], (128, 128))
            lower[pl.ds(r * 128, 128), :] = jnp.transpose(wide)

    def ring(buf, ssem, rsem, me, towards, side, s, piece):
        sign = 1 - 2 * side
        src = lax.rem(me - sign * (s - 1) + 8, 8)
        part = pl.ds(4 * piece, 4)
        return remote(buf.at[src, part], buf.at[src, part], ssem.at[side, s, piece], rsem.at[side, s, piece], towards(sign))

    def along_z(sign):
        return at(z + sign, y)

    def along_y(sign):
        return at(z, y + sign)

    def ring_step(stream, side, s, piece, last):
        buf, ssem, rsem, me, towards = stream
        sign = 1 - 2 * side
        if s > 1 and s - 1 <= last:
            src = lax.rem(me - sign * (s - 1) + 8, 8)
            part = pl.ds(4 * piece, 4)
            remote(buf.at[src, part], buf.at[src, part], ssem.at[side, s - 1, piece],
                   rsem.at[side, s - 1, piece], towards(sign)).wait_recv()
        if s <= last:
            go(ring(*stream, side, s, piece))

    def kv_step(s, piece):
        for side in (0, 1):
            for stream in ((wk, k2s, k2r, z, along_z), (wv, v2s, v2r, y, along_y)):
                ring_step(stream, side, s, piece, 4 if side == piece else 3)

    def q_step(h, s, piece):
        for side in (1, 0):
            ring_step((wq.at[h], q2s.at[h], q2r.at[h], z, along_z), side, s, piece, 4 if side == 1 else 3)

    def kv_project():
        own_tok.wait()
        acc[...] = jnp.zeros_like(acc)

        def kv_dot(i, carry):
            ws = []
            for zz in (0, 1):
                for yy in range(8):
                    kk = wk[2 * i + zz, yy].astype(F32)
                    vv = wv[yy, 2 * i + zz].astype(F32)
                    ws.append(jnp.concatenate([kk, vv], axis=1))
            w = jnp.concatenate(ws, axis=0).astype(BF)
            t = tok[:, pl.ds(pl.multiple_of(i * 1152, 1152), 1152)]
            acc[...] += jnp.dot(t, w, preferred_element_type=F32)
            return carry

        lax.fori_loop(0, 4, kv_dot, 0)
        kvs[0] = acc[...].astype(BF)

    right = (lax.rem(c + 1, 64), f)
    left = (lax.rem(c + 63, 64), f)

    def halo(src_slot, dst_slot, piece, dev, extra=False):
        part = pl.ds(256 * piece, 256)
        return remote(kvs.at[src_slot, part], kvs.at[dst_slot, part], hs.at[0 if extra else dst_slot, piece],
                      hr.at[dst_slot, piece], dev)

    def halo_start(piece):
        go(halo(0, 8, piece, at(z + 1, y)))

        @pl.when(y != 7)
        def _():
            halo(0, 1, piece, at(z, y + 1)).start()

        @pl.when(y == 0)
        def _():
            halo(0, 7, piece, at(z, y - 1)).start()

    def halo_step(slot, piece):
        halo(slot, slot, piece, at(z, y)).wait_recv()
        if slot == 8:
            @pl.when(y == 7)
            def _():
                halo(8, 1, piece, at(z, y + 1)).start()

            @pl.when(y != 0)
            def _():
                halo(8, 7, piece, at(z, y - 1)).start()
        elif slot < 3:
            go(halo(slot, slot + 1, piece, right))
        elif slot == 3:
            @pl.when(y != 7)
            def _():
                halo(3, 4, piece, right).start()
        elif slot == 4:
            @pl.when(y == 6)
            def _():
                halo(4, 5, piece, right, True).start()
        elif slot == 5:
            @pl.when(y == 1)
            def _():
                halo(5, 4, piece, left, True).start()
        elif slot == 6:
            @pl.when(y != 0)
            def _():
                halo(6, 5, piece, left).start()
        else:
            go(halo(slot, slot - 1, piece, left))

    def halo_end():
        for piece in (0, 1):
            halo(0, 1, piece, right).wait_send()
            halo(0, 7, piece, left).wait_send()

            @pl.when(y != 7)
            def _():
                halo(0, 4, piece, right).wait_send()

            @pl.when(y != 0)
            def _():
                halo(0, 5, piece, left).wait_send()

            @pl.when((y == 1) | (y == 6))
            def _():
                halo(0, 4, piece, left, True).wait_send()

    lane_id = lax.broadcasted_iota(jnp.int32, (1, 128), 1)

    def attend(h, slot):
        base = (c - slot) * SHARD

        def tile(rows):
            s = lax.dot_general(q[h, rows, :], kvs[slot, :, pl.ds(0, HD)],
                                (((1,), (1,)), ((), ())), preferred_element_type=F32)
            low = lower[rows, :] - base
            den = dacc[h, rows, :]
            parts = []
            for t in range(4):
                e = jnp.exp2(jnp.tanh(s[:, t * 128:(t + 1) * 128] * IN_SCALE) * OUT_SCALE)
                e = jnp.where(lane_id + t * 128 >= low, e, 0.0)
                den += e
                parts.append(e.astype(BF))
            dacc[h, rows, :] = den
            p = jnp.concatenate(parts, axis=1)
            oacc[h, rows, :] += jnp.dot(p, kvs[slot, :, pl.ds(HD, HD)], preferred_element_type=F32)

        tile(pl.ds(0, SHARD))

    def attend_own(h):
        for i in range(4):
            n = i + 1
            rows = pl.ds(i * 128, 128)
            s = lax.dot_general(q[h, rows, :], kvs[0, pl.ds(0, n * 128), pl.ds(0, HD)],
                                (((1,), (1,)), ((), ())), preferred_element_type=F32)
            low = lower[rows, :] - c * SHARD
            den = dacc[h, rows, :]
            parts = []
            for t in range(n):
                e = jnp.exp2(jnp.tanh(s[:, t * 128:(t + 1) * 128] * IN_SCALE) * OUT_SCALE)
                seen = lane_id + t * 128 >= low
                if t == i:
                    seen = seen & (lane_id <= lax.broadcasted_iota(jnp.int32, (128, 128), 0))
                e = jnp.where(seen, e, 0.0)
                den += e
                parts.append(e.astype(BF))
            dacc[h, rows, :] = den
            p = jnp.concatenate(parts, axis=1) if n > 1 else parts[0]
            oacc[h, rows, :] += jnp.dot(p, kvs[0, pl.ds(0, n * 128), pl.ds(HD, HD)], preferred_element_type=F32)

    def q_dot(h):
        cols = pl.ds(0, HD)
        acc[:, cols] = jnp.zeros((SHARD, HD), F32)

        def step(i, carry):
            ws = []
            for zz in (0, 1):
                for yy in range(8):
                    ws.append(wq[h, 2 * i + zz, yy].astype(F32))
            w = jnp.concatenate(ws, axis=0).astype(BF)
            t = tok[:, pl.ds(pl.multiple_of(i * 1152, 1152), 1152)]
            acc[:, cols] += jnp.dot(t, w, preferred_element_type=F32)
            return carry

        lax.fori_loop(0, 4, step, 0)
        q[h] = acc[:, cols].astype(BF)

    def finish(h):
        den = jnp.sum(dacc[h], axis=1, keepdims=True)
        att[h] = (oacc[h] / den).astype(BF)
        for d in range(1, NF):
            peer = lax.rem(f + d, NF)
            rows = pl.ds(pl.multiple_of(peer * 64, 64), 64)
            cols = pl.ds(pl.multiple_of(f * 256 + h * HD, HD), HD)
            go(remote(att.at[h, rows], out_ref.at[:, cols], as_.at[h, d], ar.at[h, d], (c, peer)))
        rows = pl.ds(pl.multiple_of(f * 64, 64), 64)
        cols = pl.ds(pl.multiple_of(f * 256 + h * HD, HD), HD)
        pltpu.make_async_copy(att.at[h, rows], out_ref.at[:, cols], loc_sem.at[h]).start()

    def finish_wait(h):
        rows = pl.ds(pl.multiple_of(f * 64, 64), 64)
        for d in range(1, NF):
            peer = lax.rem(f - d + NF, NF)
            cols = pl.ds(pl.multiple_of(peer * 256 + h * HD, HD), HD)
            remote(att.at[h, rows], out_ref.at[:, cols], as_.at[h, d], ar.at[h, d], (c, f)).wait_recv()
        cols = pl.ds(pl.multiple_of(f * 256 + h * HD, HD), HD)
        pltpu.make_async_copy(att.at[h, rows], out_ref.at[:, cols], loc_sem.at[h]).wait()

    def attend_run(run):
        if len(run) == 1:
            attend(*run[0])
            return

        def pick(i, values):
            value = values[-1]
            for n in range(len(values) - 1):
                value = jnp.where(i == n, values[n], value)
            return value

        def step(i, x):
            attend(pick(i, [h for h, _ in run]), pick(i, [slot for _, slot in run]))
            return x

        lax.fori_loop(0, len(run), step, 0)

    steps = {"S": first_slabs, "W": first_slabs_wait, "F": q_first, "G": q_first_done, "K": kv_step,
             "Q": q_step, "D": bounds, "P": kv_project, "B": halo_start, "H": halo_step,
             "R": q_dot, "O": attend_own}
    left_of = {h: sum(t[:2] == ("A", h) for t in ORDER) for h in (0, 1)}
    i = 0
    while i < len(ORDER):
        name, *args = ORDER[i]
        if name != "A":
            steps[name](*args)
            i += 1
            continue
        run = []
        while i < len(ORDER) and ORDER[i][0] == "A" and all(left_of.values()) | (not run):
            run.append(ORDER[i][1:])
            left_of[ORDER[i][1]] -= 1
            i += 1
        attend_run(run)
        for h in (0, 1):
            if left_of[h] == 0 and any(a == h for a, _ in run):
                finish(h)

    for copy in sent:
        copy.wait_send()
    halo_end()
    finish_wait(0)
    finish_wait(1)


def on_device(tokens, w_query, w_key, w_value, doc_ids):
    docs = doc_ids.reshape(256, 128)
    hbm = pl.BlockSpec(memory_space=pl.ANY)
    dma = pltpu.SemaphoreType.DMA
    return pl.pallas_call(
        kernel,
        out_shape=jax.ShapeDtypeStruct((64, 2048), BF),
        in_specs=[hbm] * 5,
        out_specs=hbm,
        scratch_shapes=[
            pltpu.VMEM((256, 128), jnp.int32),
            pltpu.VMEM((SHARD, D), BF),
            pltpu.VMEM((8, 8, SLAB, HD), BF),
            pltpu.VMEM((8, 8, SLAB, HD), BF),
            pltpu.VMEM((2, 8, 8, SLAB, HD), BF),
            pltpu.VMEM((9, SHARD, 2 * HD), BF),
            pltpu.VMEM((2, SHARD, HD), BF),
            pltpu.VMEM((SHARD, 2 * HD), F32),
            pltpu.VMEM((2, SHARD, HD), F32),
            pltpu.VMEM((2, SHARD, HD), F32),
            pltpu.VMEM((SHARD, HD), jnp.int32),
            pltpu.VMEM((2, SHARD, HD), BF),
            dma((6,)),
            dma((8,)), dma((8,)), dma((8,)), dma((8,)),
            dma((2, 5, 2)), dma((2, 5, 2)), dma((2, 5, 2)), dma((2, 5, 2)),
            dma((2, 5)), dma((2, 5)),
            dma((2, 2, 5, 2)), dma((2, 2, 5, 2)),
            dma((9, 2)), dma((9, 2)),
            dma((2, 8)), dma((2, 8)),
        ],
        compiler_params=pltpu.CompilerParams(
            collective_id=0, has_side_effects=True, vmem_limit_bytes=63 << 20),
        cost_estimate=pl.CostEstimate(flops=5 * 10 ** 9, bytes_accessed=10 ** 7, transcendentals=9 * 10 ** 6),
    )(tokens, w_query, w_key, w_value, docs)


def solution(mesh):
    return jax.shard_map(
        on_device,
        mesh=mesh,
        in_specs=(P("ctx", None), P("ctx", "fsdp"), P("ctx", "fsdp"), P("ctx", "fsdp"), P()),
        out_specs=P(("ctx", "fsdp"), None),
        check_vma=False,
    )
```

```python
import functools
import math

import jax
import jax.numpy as jnp
from jax import lax
from jax.experimental import pallas as pl
from jax.experimental.pallas import tpu as pltpu
from jax.sharding import PartitionSpec as P

MESH = pl.DeviceIdType.MESH
HD = 128
WINDOW = 4096
SHARD = 512
K_PIECES, Q_PIECES, H_PIECES = 2, 2, 4
H_ROWS = SHARD // H_PIECES
D = 4608
SLAB = 72
NZ = NY = 8
NF = 8
BF = jnp.bfloat16
F32 = jnp.float32

query_scale = 144.0 ** (-0.5)
score_cap = 50.0
IN_SCALE = query_scale / score_cap
OUT_SCALE = score_cap * math.log2(math.e)

ORDER = (
    ('S',), ('F', 1, 0), ('F', 1, 1), ('F', 2, 0), ('F', 2, 1), ('W',), ('K', 1, 1, 0, 0), ('K', 1, 1, 0, 1),
    ('K', 1, 1, 1, 0), ('K', 1, 1, 1, 1), ('F', 3, 0), ('F', 3, 1), ('K', 1, 0, 0, 0), ('K', 1, 0, 0, 1),
    ('K', 1, 0, 1, 0), ('K', 1, 0, 1, 1), ('K', 2, 1, 0, 0), ('K', 2, 1, 0, 1), ('K', 2, 1, 1, 0),
    ('K', 2, 1, 1, 1), ('K', 2, 0, 0, 0), ('K', 2, 0, 0, 1), ('K', 2, 0, 1, 0), ('K', 2, 0, 1, 1),
    ('F', 4, 0), ('K', 3, 1, 0, 0), ('K', 3, 1, 0, 1), ('K', 3, 1, 1, 0), ('K', 3, 1, 1, 1),
    ('K', 3, 0, 0, 0), ('K', 3, 0, 0, 1), ('K', 3, 0, 1, 0), ('K', 3, 0, 1, 1), ('G',), ('Q', 0, 1, 1, 1),
    ('Q', 0, 1, 1, 0), ('Q', 0, 1, 0, 1), ('Q', 0, 1, 0, 0), ('K', 4, 1, 0, 0), ('K', 4, 1, 0, 1),
    ('K', 4, 1, 1, 0), ('K', 4, 1, 1, 1), ('Q', 1, 1, 0, 1), ('Q', 1, 1, 0, 0), ('K', 4, 0, 0, 0),
    ('K', 4, 0, 0, 1), ('K', 4, 0, 1, 0), ('K', 4, 0, 1, 1), ('Q', 0, 2, 0, 1), ('Q', 0, 2, 0, 0),
    ('K', 5, 1, 1, 0), ('K', 5, 1, 1, 1), ('Q', 1, 1, 1, 1), ('Q', 1, 1, 1, 0), ('K', 5, 0, 0, 0),
    ('K', 5, 0, 0, 1), ('Q', 0, 2, 1, 1), ('Q', 0, 2, 1, 0), ('P',), ('B', 0), ('B', 1), ('Q', 1, 2, 1, 1),
    ('Q', 1, 2, 1, 0), ('B', 2), ('B', 3), ('Q', 0, 3, 0, 1), ('Q', 0, 3, 0, 0), ('H', 8, 0), ('H', 8, 1),
    ('Q', 0, 4, 0, 1), ('Q', 0, 4, 0, 0), ('Q', 0, 3, 1, 1), ('Q', 0, 3, 1, 0), ('Q', 1, 3, 1, 1),
    ('Q', 1, 3, 1, 0), ('Q', 1, 2, 0, 1), ('Q', 1, 2, 0, 0), ('D',), ('H', 8, 2), ('H', 8, 3), ('H', 1, 0),
    ('H', 1, 1), ('H', 7, 0), ('H', 7, 1), ('Q', 0, 4, 1, 1), ('Q', 0, 4, 1, 0), ('Q', 1, 4, 1, 1),
    ('Q', 1, 4, 1, 0), ('Q', 1, 3, 0, 1), ('Q', 1, 3, 0, 0), ('Q', 0, 5, 0, 1), ('H', 7, 2), ('H', 7, 3),
    ('H', 1, 2), ('H', 1, 3), ('Q', 0, 5, 1, 1), ('R', 0), ('O', 0), ('H', 6, 0), ('H', 6, 1), ('A', 0, 8),
    ('H', 2, 0), ('H', 2, 1), ('A', 0, 1), ('Q', 1, 4, 0, 1), ('Q', 1, 4, 0, 0), ('H', 6, 2), ('H', 6, 3),
    ('A', 0, 7), ('H', 2, 2), ('H', 2, 3), ('A', 0, 6), ('Q', 1, 5, 1, 1), ('A', 0, 2), ('H', 3, 0),
    ('H', 3, 1), ('Q', 1, 5, 0, 1), ('R', 1), ('O', 1), ('H', 5, 0), ('H', 5, 1), ('A', 1, 6), ('A', 1, 8),
    ('H', 3, 2), ('H', 3, 3), ('A', 1, 3), ('A', 1, 2), ('H', 4, 0), ('H', 4, 1), ('A', 1, 7), ('H', 5, 2),
    ('H', 5, 3), ('A', 1, 1), ('A', 1, 5), ('A', 0, 3), ('H', 4, 2), ('H', 4, 3), ('A', 1, 4), ('A', 0, 4),
    ('A', 0, 5),
)


def kernel(tok_hbm, wq_hbm, wk_hbm, wv_hbm, doc_hbm, out_ref,
           doc_ref, tok, wk, wv, wq, kvs, q, acc, oacc, dacc, lower, att,
           loc_sem, k1s, k1r, v1s, v1r, k2s, k2r, v2s, v2r, q1s, q1r, q2s, q2r,
           hs, hr, as_, ar):
    c = lax.axis_index("ctx")
    f = lax.axis_index("fsdp")
    z, y = c // NY, c % NY

    def at(zz, yy):
        return (lax.rem(zz + NZ, NZ) * NY + lax.rem(yy + NY, NY), f)

    def remote(src, dst, ssem, rsem, dev):
        return pltpu.make_async_remote_copy(
            src_ref=src, dst_ref=dst, send_sem=ssem, recv_sem=rsem,
            device_id=dev, device_id_type=MESH)

    sent = []

    def go(copy):
        copy.start()
        sent.append(copy)

    own_q0 = pltpu.make_async_copy(wq_hbm.at[:, pl.ds(0, HD)], wq.at[0, z, y], loc_sem.at[0])
    own_q1 = pltpu.make_async_copy(wq_hbm.at[:, pl.ds(HD, HD)], wq.at[1, z, y], loc_sem.at[1])
    own_k = pltpu.make_async_copy(wk_hbm, wk.at[z, y], loc_sem.at[2])
    own_v = pltpu.make_async_copy(wv_hbm, wv.at[y, z], loc_sem.at[3])
    own_doc = pltpu.make_async_copy(doc_hbm, doc_ref, loc_sem.at[5])
    own_tok = pltpu.make_async_copy(tok_hbm, tok, loc_sem.at[4])
    own_k.start()
    own_v.start()
    own_q0.start()
    own_q1.start()
    own_doc.start()
    own_tok.start()

    bar = pltpu.get_barrier_semaphore()
    peers = [at(z, y + d) for d in range(1, NY)]
    peers += [at(z + d, y) for d in range(1, NZ)]
    peers += [(c, lax.rem(f + d, NF)) for d in range(1, NF)]
    for p in peers:
        pl.semaphore_signal(bar, inc=1, device_id=p, device_id_type=MESH)

    @pl.when(y == NY - 1)
    def _():
        pl.semaphore_signal(bar, inc=1, device_id=at(z + 1, 0), device_id_type=MESH)

    @pl.when(y == 0)
    def _():
        pl.semaphore_signal(bar, inc=1, device_id=at(z - 1, NY - 1), device_id_type=MESH)

    edge = jnp.where((y == 0) | (y == NY - 1), 1, 0)
    pl.semaphore_wait(bar, len(peers) + edge)

    order = [1, 7, 2, 6, 3, 5, 4]

    def first_slabs():
        own_k.wait()
        own_v.wait()
        for d in order:
            go(remote(wk.at[z, y], wk.at[z, y], k1s.at[d], k1r.at[d], at(z, y + d)))
            go(remote(wv.at[y, z], wv.at[y, z], v1s.at[d], v1r.at[d], at(z + d, y)))
        own_q0.wait()
        own_q1.wait()
        oacc[...] = jnp.zeros_like(oacc)
        dacc[...] = jnp.zeros_like(dacc)

    def first_slabs_wait():
        for d in order:
            src = lax.rem(y - d + NY, NY)
            remote(wk.at[z, src], wk.at[z, src], k1s.at[d], k1r.at[d], at(z, y)).wait_recv()
            src = lax.rem(z - d + NZ, NZ)
            remote(wv.at[y, src], wv.at[y, src], v1s.at[d], v1r.at[d], at(z, y)).wait_recv()

    def q_first(s, side):
        sign = 1 - 2 * side
        src = lax.rem(y - sign * (s - 1) + NY, NY)
        if s > 1:
            remote(wq.at[:, z, src], wq.at[:, z, src], q1s.at[side, s - 1], q1r.at[side, s - 1], at(z, y)).wait_recv()
        go(remote(wq.at[:, z, src], wq.at[:, z, src], q1s.at[side, s], q1r.at[side, s], at(z, y + sign)))

    def q_first_done():
        for side, s in ((0, 4), (1, 3)):
            sign = 1 - 2 * side
            src = lax.rem(y - sign * s + NY, NY)
            remote(wq.at[:, z, src], wq.at[:, z, src], q1s.at[side, s], q1r.at[side, s], at(z, y)).wait_recv()

    def bounds():
        own_doc.wait()
        docs = doc_ref[...]
        half = doc_ref[pl.ds(pl.multiple_of((c // 2) * 8, 8), 8), :]
        starts = jnp.zeros((8, 128), jnp.int32)
        for n in range(1, 16):
            begin = jnp.sum((docs < n).astype(jnp.int32))
            starts = jnp.where(half == n, begin, starts)
        row = lax.broadcasted_iota(jnp.int32, (8, 128), 0)
        lane = lax.broadcasted_iota(jnp.int32, (8, 128), 1)
        pos = (c // 2) * (2 * SHARD) + row * 128 + lane
        starts = jnp.maximum(starts, pos - (WINDOW - 1))
        starts = jnp.where(c % 2 == 0, starts, jnp.concatenate([starts[4:8], starts[0:4]], axis=0))
        for r in range(4):
            wide = jnp.broadcast_to(starts[r:r + 1, :], (128, 128))
            lower[pl.ds(r * 128, 128), :] = jnp.transpose(wide)

    def along_z(sign):
        return at(z + sign, y)

    def along_y(sign):
        return at(z, y + sign)

    def ring_step(stream, pieces, side, s, piece, last):
        buf, ssem, rsem, me, towards = stream
        sign = 1 - 2 * side
        part = pl.ds(8 // pieces * piece, 8 // pieces)
        if s > 1:
            src = lax.rem(me - sign * (s - 1) + 8, 8)
            remote(buf.at[src, part], buf.at[src, part], ssem.at[side, s - 1, piece],
                   rsem.at[side, s - 1, piece], towards(sign)).wait_recv()
        if s <= last:
            src = lax.rem(me - sign * (s - 1) + 8, 8)
            go(remote(buf.at[src, part], buf.at[src, part], ssem.at[side, s, piece],
                      rsem.at[side, s, piece], towards(sign)))

    def kv_step(s, piece, side, stream):
        last = 4 if (side == 0) == (piece < K_PIECES // 2) else 3
        streams = ((wk, k2s, k2r, z, along_z), (wv, v2s, v2r, y, along_y))
        ring_step(streams[stream], K_PIECES, side, s, piece, last)

    def q_step(h, s, piece, side):
        ring_step((wq.at[h], q2s.at[h], q2r.at[h], z, along_z), Q_PIECES, side, s, piece, 4 if side == 1 else 3)

    def kv_project():
        own_tok.wait()
        acc[...] = jnp.zeros_like(acc)

        def kv_dot(i, carry):
            ws = []
            for zz in (0, 1):
                for yy in range(8):
                    kk = wk[2 * i + zz, yy].astype(F32)
                    vv = wv[yy, 2 * i + zz].astype(F32)
                    ws.append(jnp.concatenate([kk, vv], axis=1))
            w = jnp.concatenate(ws, axis=0).astype(BF)
            t = tok[:, pl.ds(pl.multiple_of(i * 1152, 1152), 1152)]
            acc[...] += jnp.dot(t, w, preferred_element_type=F32)
            return carry

        lax.fori_loop(0, 4, kv_dot, 0)
        kvs[0] = acc[...].astype(BF)

    right = (lax.rem(c + 1, 64), f)
    left = (lax.rem(c + 63, 64), f)

    def halo(src_slot, dst_slot, piece, dev, extra=False):
        part = pl.ds(H_ROWS * piece, H_ROWS)
        return remote(kvs.at[src_slot, part], kvs.at[dst_slot, part], hs.at[0 if extra else dst_slot, piece],
                      hr.at[dst_slot, piece], dev)

    def halo_start(piece):
        go(halo(0, 8, piece, at(z + 1, y)))

        @pl.when(y != 7)
        def _():
            halo(0, 1, piece, at(z, y + 1)).start()

        @pl.when(y == 0)
        def _():
            halo(0, 7, piece, at(z, y - 1)).start()

    def halo_step(slot, piece):
        halo(slot, slot, piece, at(z, y)).wait_recv()
        if slot == 8:
            @pl.when(y == 7)
            def _():
                halo(8, 1, piece, at(z, y + 1)).start()

            @pl.when(y != 0)
            def _():
                halo(8, 7, piece, at(z, y - 1)).start()
        elif slot < 3:
            go(halo(slot, slot + 1, piece, right))
        elif slot == 3:
            @pl.when(y != 7)
            def _():
                halo(3, 4, piece, right).start()
        elif slot == 4:
            @pl.when(y == 6)
            def _():
                halo(4, 5, piece, right, True).start()
        elif slot == 5:
            @pl.when(y == 1)
            def _():
                halo(5, 4, piece, left, True).start()
        elif slot == 6:
            @pl.when(y != 0)
            def _():
                halo(6, 5, piece, left).start()
        else:
            go(halo(slot, slot - 1, piece, left))

    def halo_end():
        for piece in range(H_PIECES):
            halo(0, 1, piece, right).wait_send()
            halo(0, 7, piece, left).wait_send()

            @pl.when(y != 7)
            def _():
                halo(0, 4, piece, right).wait_send()

            @pl.when(y != 0)
            def _():
                halo(0, 5, piece, left).wait_send()

            @pl.when((y == 1) | (y == 6))
            def _():
                halo(0, 4, piece, left, True).wait_send()

    lane_id = lax.broadcasted_iota(jnp.int32, (1, 128), 1)

    def attend(h, slot):
        base = (c - slot) * SHARD

        def tile(rows):
            s = lax.dot_general(q[h, rows, :], kvs[slot, :, pl.ds(0, HD)],
                                (((1,), (1,)), ((), ())), preferred_element_type=F32)
            low = lower[rows, :] - base
            den = dacc[h, rows, :]
            parts = []
            for t in range(4):
                e = jnp.exp2(jnp.tanh(s[:, t * 128:(t + 1) * 128] * IN_SCALE) * OUT_SCALE)
                e = jnp.where(lane_id + t * 128 >= low, e, 0.0)
                den += e
                parts.append(e.astype(BF))
            dacc[h, rows, :] = den
            p = jnp.concatenate(parts, axis=1)
            oacc[h, rows, :] += jnp.dot(p, kvs[slot, :, pl.ds(HD, HD)], preferred_element_type=F32)

        tile(pl.ds(0, SHARD))

    def attend_own(h):
        for i in range(4):
            n = i + 1
            rows = pl.ds(i * 128, 128)
            s = lax.dot_general(q[h, rows, :], kvs[0, pl.ds(0, n * 128), pl.ds(0, HD)],
                                (((1,), (1,)), ((), ())), preferred_element_type=F32)
            low = lower[rows, :] - c * SHARD
            den = dacc[h, rows, :]
            parts = []
            for t in range(n):
                e = jnp.exp2(jnp.tanh(s[:, t * 128:(t + 1) * 128] * IN_SCALE) * OUT_SCALE)
                seen = lane_id + t * 128 >= low
                if t == i:
                    seen = seen & (lane_id <= lax.broadcasted_iota(jnp.int32, (128, 128), 0))
                e = jnp.where(seen, e, 0.0)
                den += e
                parts.append(e.astype(BF))
            dacc[h, rows, :] = den
            p = jnp.concatenate(parts, axis=1) if n > 1 else parts[0]
            oacc[h, rows, :] += jnp.dot(p, kvs[0, pl.ds(0, n * 128), pl.ds(HD, HD)], preferred_element_type=F32)

    def q_dot(h):
        cols = pl.ds(0, HD)
        acc[:, cols] = jnp.zeros((SHARD, HD), F32)

        def step(i, carry):
            ws = []
            for zz in (0, 1):
                for yy in range(8):
                    ws.append(wq[h, 2 * i + zz, yy].astype(F32))
            w = jnp.concatenate(ws, axis=0).astype(BF)
            t = tok[:, pl.ds(pl.multiple_of(i * 1152, 1152), 1152)]
            acc[:, cols] += jnp.dot(t, w, preferred_element_type=F32)
            return carry

        lax.fori_loop(0, 4, step, 0)
        q[h] = acc[:, cols].astype(BF)

    def finish(h):
        den = jnp.sum(dacc[h], axis=1, keepdims=True)
        att[h] = (oacc[h] / den).astype(BF)
        for d in range(1, NF):
            peer = lax.rem(f + d, NF)
            rows = pl.ds(pl.multiple_of(peer * 64, 64), 64)
            cols = pl.ds(pl.multiple_of(f * 256 + h * HD, HD), HD)
            go(remote(att.at[h, rows], out_ref.at[:, cols], as_.at[h, d], ar.at[h, d], (c, peer)))
        rows = pl.ds(pl.multiple_of(f * 64, 64), 64)
        cols = pl.ds(pl.multiple_of(f * 256 + h * HD, HD), HD)
        pltpu.make_async_copy(att.at[h, rows], out_ref.at[:, cols], loc_sem.at[h]).start()

    def finish_wait(h):
        rows = pl.ds(pl.multiple_of(f * 64, 64), 64)
        for d in range(1, NF):
            peer = lax.rem(f - d + NF, NF)
            cols = pl.ds(pl.multiple_of(peer * 256 + h * HD, HD), HD)
            remote(att.at[h, rows], out_ref.at[:, cols], as_.at[h, d], ar.at[h, d], (c, f)).wait_recv()
        cols = pl.ds(pl.multiple_of(f * 256 + h * HD, HD), HD)
        pltpu.make_async_copy(att.at[h, rows], out_ref.at[:, cols], loc_sem.at[h]).wait()

    def attend_run(run):
        if len(run) == 1:
            attend(*run[0])
            return

        def pick(i, values):
            value = values[-1]
            for n in range(len(values) - 1):
                value = jnp.where(i == n, values[n], value)
            return value

        def step(i, x):
            attend(pick(i, [h for h, _ in run]), pick(i, [slot for _, slot in run]))
            return x

        lax.fori_loop(0, len(run), step, 0)

    steps = {"S": first_slabs, "W": first_slabs_wait, "F": q_first, "G": q_first_done, "K": kv_step,
             "Q": q_step, "D": bounds, "P": kv_project, "B": halo_start, "H": halo_step,
             "R": q_dot, "O": attend_own}
    left_of = {h: sum(t[:2] == ("A", h) for t in ORDER) for h in (0, 1)}
    i = 0
    while i < len(ORDER):
        name, *args = ORDER[i]
        if name == "H" and args[0] in (1, 2, 3) and args[1] == H_PIECES - 1:
            while len(sent) > 40:
                sent.pop(0).wait_send()
        if name != "A":
            steps[name](*args)
            i += 1
            continue
        run = []
        while i < len(ORDER) and ORDER[i][0] == "A" and all(left_of.values()) | (not run):
            run.append(ORDER[i][1:])
            left_of[ORDER[i][1]] -= 1
            i += 1
        attend_run(run)
        for h in (0, 1):
            if left_of[h] == 0 and any(a == h for a, _ in run):
                finish(h)

    for copy in sent:
        copy.wait_send()
    halo_end()
    finish_wait(0)
    finish_wait(1)


def on_device(tokens, w_query, w_key, w_value, doc_ids):
    docs = doc_ids.reshape(256, 128)
    hbm = pl.BlockSpec(memory_space=pl.ANY)
    dma = pltpu.SemaphoreType.DMA
    return pl.pallas_call(
        kernel,
        out_shape=jax.ShapeDtypeStruct((64, 2048), BF),
        in_specs=[hbm] * 5,
        out_specs=hbm,
        scratch_shapes=[
            pltpu.VMEM((256, 128), jnp.int32),
            pltpu.VMEM((SHARD, D), BF),
            pltpu.VMEM((8, 8, SLAB, HD), BF),
            pltpu.VMEM((8, 8, SLAB, HD), BF),
            pltpu.VMEM((2, 8, 8, SLAB, HD), BF),
            pltpu.VMEM((9, SHARD, 2 * HD), BF),
            pltpu.VMEM((2, SHARD, HD), BF),
            pltpu.VMEM((SHARD, 2 * HD), F32),
            pltpu.VMEM((2, SHARD, HD), F32),
            pltpu.VMEM((2, SHARD, HD), F32),
            pltpu.VMEM((SHARD, HD), jnp.int32),
            pltpu.VMEM((2, SHARD, HD), BF),
            dma((6,)),
            dma((8,)), dma((8,)), dma((8,)), dma((8,)),
            dma((2, 5, K_PIECES)), dma((2, 5, K_PIECES)), dma((2, 5, K_PIECES)), dma((2, 5, K_PIECES)),
            dma((2, 5)), dma((2, 5)),
            dma((2, 2, 5, Q_PIECES)), dma((2, 2, 5, Q_PIECES)),
            dma((9, H_PIECES)), dma((9, H_PIECES)),
            dma((2, 8)), dma((2, 8)),
        ],
        compiler_params=pltpu.CompilerParams(
            collective_id=0, has_side_effects=True, vmem_limit_bytes=63 << 20),
        cost_estimate=pl.CostEstimate(flops=5 * 10 ** 9, bytes_accessed=10 ** 7, transcendentals=9 * 10 ** 6),
    )(tokens, w_query, w_key, w_value, docs)


def solution(mesh):
    return jax.shard_map(
        on_device,
        mesh=mesh,
        in_specs=(P("ctx", None), P("ctx", "fsdp"), P("ctx", "fsdp"), P("ctx", "fsdp"), P()),
        out_specs=P(("ctx", "fsdp"), None),
        check_vma=False,
    )
```
